128 devices in a mesh: dp: 8 (over z, core), tensor: 16 (over y, x).
Axes of the slice: x: 4, y: 4, z: 4, core: 2. Of those that a mesh axis runs over, the one named last changes fastest.
Arguments:
- tokens: bfloat16 [10240, 4096], P('dp'), may hold values from -6 to 6
- gate_weight: bfloat16 [4096, 14336], P(None, 'tensor'), may hold values from -0.125 to 0.125
- up_values: bfloat16 [10240, 14336], P('dp', 'tensor'), may hold values from -6 to 6
- hidden_grad: bfloat16 [10240, 14336], P('dp', 'tensor'), may hold values from -48 to 48
- log_ratios: float32 [64, 2], P('dp'), may hold values from -60 to 60
- q_factors: float32 [14336, 32], P('tensor'), may hold values from -6 to 6
- error_feedback: bfloat16 [8, 4096, 14336], P('dp', None, 'tensor'), may hold values from -12 to 12
Outputs:
- token_grad: bfloat16 [10240, 4096], P('dp', 'tensor')
- q_next: float32 [14336, 32], P('tensor')
- error_next: bfloat16 [8, 4096, 14336], P('dp', None, 'tensor')
The draws below stay inside these ranges and needn't reach their ends.
All inputs are finite; a program needn't handle non-finite values.
Results may differ from the reference program's by a relative error of at most 0.019.
Values may be sent and summed in bfloat16 or wider, within the bound.
No kernel may reach another device: no remote copies, remote signals or barrier semaphores. Data moves between devices by JAX's collectives and lax.ppermute only.
A program may use at most 192 MiB of HBM per device.

```python
import jax
import jax.numpy as jnp
from jax import lax

D = 4096
FF = 14336
R = 32
LEN = 80
PAIRS_DEV = 8
PAIRS = 64
ROWS = 10240
N_DP = 8
N_TENSOR = 16


def strengthened(drawn, key, source, target, blocks, factor):
    owner, partner = [(jnp.arange(drawn.shape[position]) // (drawn.shape[position] // blocks)).reshape([-1 if axis == position else 1 for axis in range(drawn.ndim)]) for position in (source, target)]
    chosen = jax.random.permutation(key, blocks)[partner]
    strong = (owner == chosen) | (owner == (partner + blocks // 2) % blocks)
    return jnp.where(strong, factor * drawn, drawn)


def block_levels(rng, extent, cuts, smallest, top_value):
    def one(dim, shards_of):
        steps = jax.random.uniform(jax.random.fold_in(jax.random.fold_in(rng, 6), dim), (shards_of,), jnp.float32, smallest / len(cuts), top_value / len(cuts))
        return jnp.repeat(jnp.exp(steps), extent[dim] // shards_of).reshape((-1,) + (1,) * (len(extent) - dim - 1))

    factor_of = one(*cuts[0])
    for cut in cuts[1:]:
        factor_of = factor_of * one(*cut)
    return factor_of


def scatter_about(key, dims, scale, most, split=(), held_as=jnp.bfloat16):
    entries = jax.random.normal(key, dims, jnp.float32) * scale
    if len(split) > 0:
        entries = block_levels(key, dims, split, -0.22, 0.18) * entries
    return jnp.clip(entries, min=-most, max=most).astype(held_as)


def bell_draw_with(stream_key, dims, scale, most, shards, heavy, kind=jnp.bfloat16):
    values = scale * jax.random.normal(stream_key, dims, jnp.float32)
    if shards:
        values = values * block_levels(stream_key, dims, shards, -0.22, 0.18)
    return jnp.clip(strengthened(values, jax.random.fold_in(stream_key, 3), *heavy), -most, most).astype(kind)


def setup_inputs(seed: int = 0) -> dict:
    streams_of = jax.random.split(jax.random.key(seed), 8)
    tokens = scatter_about(streams_of[0], (ROWS, D), 1.0, 6.0, ((0, 8),))
    gate_weight = bell_draw_with(streams_of[1], (D, FF), D ** -0.5, 0.125, ((1, 16),), (1, 0, 16, 2.0))
    up_values = scatter_about(streams_of[2], (ROWS, FF), 1.0, 6.0, ((0, 8), (1, 16)))
    hidden_grad = scatter_about(streams_of[3], (ROWS, FF), 8.0, 48.0, ((0, 8), (1, 16)))
    log_ratios = scatter_about(streams_of[4], (PAIRS, 2), 10.0, 60.0, ((0, 8),), jnp.float32)
    q_factors = scatter_about(streams_of[5], (FF, R), 1.0, 6.0, ((0, 16),), jnp.float32)
    error_feedback = scatter_about(streams_of[6], (N_DP, D, FF), 2.0, 12.0, ((0, 8), (2, 16)))
    return {"tokens": tokens, "gate_weight": gate_weight, "up_values": up_values, "hidden_grad": hidden_grad, "log_ratios": log_ratios, "q_factors": q_factors, "error_feedback": error_feedback}


dpo_beta = 0.1
highest = lax.Precision.HIGHEST

def pair_weights(log_ratios, seq_len):
    margin = dpo_beta * (log_ratios[:, 0] - log_ratios[:, 1])
    scaled = dpo_beta * jax.nn.sigmoid(-margin)
    signed = jnp.stack([-scaled, scaled], axis=1)
    spread = jnp.broadcast_to(signed[:, :, None], signed.shape + (seq_len,))
    return spread.reshape(-1)

def orthonormal(left_sum, gram_matrix):
    lower_factor = jnp.linalg.cholesky(gram_matrix)
    return lax.linalg.triangular_solve(lower_factor, left_sum, left_side=False, lower=True, transpose_a=True)

def halved(values):
    return lax.optimization_barrier(values.astype(jnp.bfloat16)).astype(jnp.float32)

def reference(tokens, gate_weight, up_values, hidden_grad, log_ratios, q_factors, error_feedback):
    shard_width = FF // N_TENSOR
    rows_replica = 2 * PAIRS_DEV * LEN
    row_weight = pair_weights(log_ratios, LEN)
    gate_pre = jnp.dot(tokens.astype(jnp.float32), gate_weight.astype(jnp.float32), preferred_element_type=jnp.float32)
    sigmoid_gate = jax.nn.sigmoid(gate_pre)
    silu_slope = sigmoid_gate * (1.0 + gate_pre * (1.0 - sigmoid_gate))
    gate_grad = (row_weight[:, None] * hidden_grad.astype(jnp.float32) * up_values.astype(jnp.float32) * silu_slope).astype(jnp.bfloat16)
    shard_ids = jnp.arange(N_TENSOR, dtype=jnp.int32)

    def input_term(running, shard_index):
        start = shard_index * shard_width
        grad_cols = lax.dynamic_slice_in_dim(gate_grad, start, shard_width, 1)
        weight_cols = lax.dynamic_slice_in_dim(gate_weight, start, shard_width, 1)
        term = lax.dot_general(grad_cols.astype(jnp.float32), weight_cols.astype(jnp.float32), (((1,), (1,)), ((), ())), preferred_element_type=jnp.float32)
        return (running + halved(term), None)
    running, _ = lax.scan(input_term, jnp.zeros((ROWS, D), jnp.float32), shard_ids)
    token_grad = running.astype(jnp.bfloat16)
    token_blocks = tokens.reshape(N_DP, rows_replica, D).astype(jnp.float32)

    def compress_shard(shard_index):
        start = shard_index * shard_width
        grad_cols = lax.dynamic_slice_in_dim(gate_grad, start, shard_width, 1).reshape(N_DP, rows_replica, shard_width).astype(jnp.float32)
        weight_grad = jnp.einsum('nrd,nrf->ndf', token_blocks, grad_cols, precision=highest)
        merged = weight_grad + lax.dynamic_slice_in_dim(error_feedback, start, shard_width, 2).astype(jnp.float32)
        merged_half = halved(merged)
        q_half = halved(lax.dynamic_slice_in_dim(q_factors, start, shard_width, 0))
        left_sum = jnp.einsum('ndf,fr->dr', merged_half, q_half, precision=highest) / N_DP
        gram_matrix = jnp.dot(left_sum.T, left_sum, precision=highest)
        left_ortho = halved(orthonormal(left_sum, gram_matrix))
        right_next = jnp.einsum('ndf,dr->fr', merged_half, left_ortho, precision=highest) / N_DP
        q_round = halved(right_next)
        approx = jnp.dot(left_ortho, q_round.T, precision=highest)
        error_block = (merged - approx[None]).astype(jnp.bfloat16)
        return (right_next, error_block)
    right_parts, error_parts = lax.map(compress_shard, shard_ids)
    q_next = right_parts.reshape(FF, R)
    error_next = jnp.transpose(error_parts, (1, 2, 0, 3)).reshape(N_DP, D, FF)
    return (token_grad, q_next, error_next)
```

```python
import functools

import jax
import jax.numpy as jnp
from jax import lax
from jax.experimental import pallas as pl
from jax.experimental.pallas import tpu as pltpu
from jax.sharding import PartitionSpec as P

bf16 = jnp.bfloat16
f32 = jnp.float32
MIB = 1 << 20

LEN = 80
PAIR = 2 * LEN
ROWS = 1280
ROWS_A = 640
D = 4096
WIDE = 896
OUT = 256
R = 32
SIDE = 4

dpo_beta = 0.1
highest = lax.Precision.HIGHEST
NT = (((1,), (1,)), ((), ()))
TN = (((0,), (0,)), ((), ()))
NN = (((1,), (0,)), ((), ()))

VM = pl.BlockSpec(memory_space=pltpu.VMEM)
SM = pl.BlockSpec(memory_space=pltpu.SMEM)
ANY = pl.BlockSpec(memory_space=pl.ANY)
HBM = pl.BlockSpec(memory_space=pltpu.HBM)


def params(mib):
    return pltpu.CompilerParams(vmem_limit_bytes=mib * MIB)


LITTLE = pl.CostEstimate(flops=1, bytes_accessed=1, transcendentals=0)


def skipping(body, n, more):
    return lambda *refs: body(*refs[:n], *refs[n + more :])


def dot(a, b, dims):
    return lax.dot_general(a, b, dims, preferred_element_type=f32)


CHUNK = 512
TILE = 2 * PAIR
DEST = SIDE * OUT
GROUPS = (("x", 0, ROWS_A), ("y", ROWS_A, ROWS - ROWS_A))
FAR, NEAR, OWN = range(3)


def position(kind, axis, place_ref):
    me = place_ref[0 if axis == "x" else 1]
    core = place_ref[2]
    return lax.rem(me + (2, 1 + 2 * core, 0)[kind], SIDE)


def weights_for(axis, c, weight_ref):
    if axis == "y":
        return weight_ref[pl.ds(pl.multiple_of(c * DEST, DEST), DEST), :]
    return jnp.concatenate(
        [weight_ref[pl.ds(feature_block(axis, j, c), OUT), :] for j in range(SIDE)], axis=0
    )


def put_terms(kind, place_ref, grad_ref, weight_ref, outs):
    for (axis, base, n), out_ref in zip(GROUPS, outs):
        weight = weights_for(axis, position(kind, axis, place_ref), weight_ref)
        term = dot(grad_ref[base : base + n, :], weight, NT).astype(bf16)
        for j in range(SIDE):
            out_ref[j] = term[:, j * OUT : (j + 1) * OUT]


def feature_block(axis, j, c):
    return pl.multiple_of((j * SIDE + c if axis == "x" else c * SIDE + j) * OUT, OUT)


def gate_grad_of(pair, ratio_ref, gate_pre, hidden, up):
    margin = dpo_beta * (ratio_ref[0, pair] - ratio_ref[1, pair])
    scaled = dpo_beta * jax.nn.sigmoid(jnp.full((PAIR, 1), -margin, f32))
    chosen = lax.broadcasted_iota(jnp.int32, (PAIR, 1), 0) < LEN
    row_weight = jnp.where(chosen, -scaled, scaled)
    s = jax.nn.sigmoid(gate_pre)
    slope = s * (1.0 + gate_pre * (1.0 - s))
    return (row_weight * hidden.astype(f32) * up.astype(f32) * slope).astype(bf16)


def gate_body(
    place_ref, ratio_ref, token_ref, weight_hbm, hidden_ref, up_ref,
    grad_ref, far_x, far_y, weight_ref, pre_ref, sems,
):
    i = pl.program_id(0)

    def chunk(k):
        at = pl.ds(k * CHUNK, CHUNK)
        return pltpu.make_async_copy(weight_hbm.at[at], weight_ref.at[at], sems.at[k])

    def finish(gate_pre):
        for p in range(TILE // PAIR):
            at = slice(p * PAIR, (p + 1) * PAIR)
            row = pl.multiple_of(i * TILE + p * PAIR, PAIR)
            grad_ref[pl.ds(row, PAIR)] = gate_grad_of(
                i * (TILE // PAIR) + p, ratio_ref, gate_pre[at], hidden_ref[at], up_ref[at]
            )

    @pl.when(i == 0)
    def _():
        for k in range(D // CHUNK):
            chunk(k).start()
        for k in range(D // CHUNK):
            chunk(k).wait()
            at = slice(k * CHUNK, (k + 1) * CHUNK)
            part = dot(token_ref[:, at], weight_ref[at], NN)
            if k == 0:
                pre_ref[...] = part
            elif k < D // CHUNK - 1:
                pre_ref[...] += part
            else:
                finish(pre_ref[...] + part)

    @pl.when(i > 0)
    def _():
        finish(dot(token_ref[...], weight_ref[...], NN))

    @pl.when(i == ROWS // TILE - 1)
    def _():
        put_terms(FAR, place_ref, grad_ref, weight_ref, (far_x, far_y))


def messages():
    return [jax.ShapeDtypeStruct((SIDE, n, OUT), bf16) for _, _, n in GROUPS]


def gate(place, ratios, tokens, weight, hidden, up):
    rows = lambda wide: pl.BlockSpec((TILE, wide), lambda i: (i, 0))
    return pl.pallas_call(
        gate_body,
        grid=(ROWS // TILE,),
        in_specs=[SM, SM, rows(D), HBM, rows(WIDE), rows(WIDE)],
        out_specs=[VM] * 4,
        out_shape=[jax.ShapeDtypeStruct((ROWS, WIDE), bf16), *messages(), pltpu.VMEM((D, WIDE), bf16)],
        scratch_shapes=[
            pltpu.VMEM((TILE, WIDE), f32),
            pltpu.SemaphoreType.DMA((D // CHUNK,)),
        ],
        compiler_params=params(24),
        cost_estimate=LITTLE,
        name="gate",
    )(place, ratios, tokens, weight, hidden, up)


def terms(kinds, place, grad, weight, after=()):
    def body(place_ref, grad_ref, weight_ref, *refs):
        outs = refs[len(after) :]
        for i, kind in enumerate(kinds):
            put_terms(kind, place_ref, grad_ref, weight_ref, outs[2 * i : 2 * i + 2])

    return pl.pallas_call(
        body,
        in_specs=[SM, VM, VM] + [ANY] * len(after),
        out_specs=[VM] * 2 * len(kinds),
        out_shape=messages() * len(kinds),
        compiler_params=params(16),
        cost_estimate=LITTLE,
        name="terms",
    )(place, grad, weight, *after)


def add(a, b, after=()):
    return pl.pallas_call(
        skipping(add_body, 2, len(after)),
        in_specs=[VM, VM] + [ANY] * len(after),
        out_specs=VM,
        out_shape=jax.ShapeDtypeStruct(a.shape, bf16),
        compiler_params=params(6),
        cost_estimate=LITTLE,
        name="add",
    )(a, b, *after)


def own_body(axis, place_ref, a_ref, b_ref, c_ref, here, other_way, this_way, far):
    me, core = place_ref[1 if axis == "x" else 0], place_ref[2]
    for d, out_ref in ((0, here), (3 - 2 * core, other_way), (1 + 2 * core, this_way), (2, far)):
        j = lax.rem(me + d, SIDE)
        out_ref[...] = (
            a_ref[j].astype(f32) + b_ref[j].astype(f32) + c_ref[j].astype(f32)
        ).astype(bf16)


def own(axis, place, a, b, c, after=()):
    n = a.shape[1]
    return pl.pallas_call(
        skipping(functools.partial(own_body, axis), 4, len(after)),
        in_specs=[SM] + [VM] * 3 + [ANY] * len(after),
        out_specs=[VM] * SIDE,
        out_shape=[jax.ShapeDtypeStruct((n, OUT), bf16)] * SIDE,
        compiler_params=params(8),
        cost_estimate=LITTLE,
        name="own_" + axis,
    )(place, a, b, c, *after)


def pack_body(a_ref, b_ref, out_ref):
    out_ref[0] = a_ref[...]
    out_ref[1] = b_ref[...]


def pack(a, b, after=()):
    return pl.pallas_call(
        skipping(pack_body, 2, len(after)),
        in_specs=[VM, VM] + [ANY] * len(after),
        out_specs=VM,
        out_shape=jax.ShapeDtypeStruct((2, *a.shape), bf16),
        compiler_params=params(4),
        cost_estimate=LITTLE,
        name="pack",
    )(a, b, *after)


def add_terms(*refs):
    out_ref = refs[-1]
    for g, (_, base, n) in enumerate(GROUPS):
        here, far, near, theirs = refs[4 * g : 4 * g + 4]
        parts = [r.astype(f32) for r in (here[...], far[...], near[0], theirs[1])]
        out_ref[base : base + n] = ((parts[0] + parts[1]) + (parts[2] + parts[3])).astype(bf16)


DEEP = 512
HALVES = 1
STEPS = D // DEEP // HALVES


def merge_body(token_ref, grad_ref, error_ref, q_ref, *refs):
    high_ref, low_ref, left_ref = refs[-3:]
    m = dot(token_ref[...], grad_ref[...], TN) + error_ref[0].astype(f32)
    high = m.astype(bf16)
    high_ref[...] = high
    low_ref[...] = (m - high.astype(f32)).astype(bf16)
    left_ref[...] = dot(q_ref[...].astype(bf16), high, NT).astype(bf16)


def merge(tokens, grad, error, q_t, before=(), after=()):
    at = STEPS if before else 0
    wide = pl.BlockSpec((DEEP, WIDE), lambda i: (at + i, 0))
    return pl.pallas_call(
        skipping(merge_body, 4 + len(before), len(after)),
        grid=(STEPS,),
        in_specs=[
            pl.BlockSpec((ROWS, DEEP), lambda i: (0, at + i)),
            VM,
            pl.BlockSpec((1, DEEP, WIDE), lambda i: (0, at + i, 0)),
            VM,
        ]
        + [ANY] * (len(before) + len(after)),
        out_specs=[wide, wide, pl.BlockSpec((R, DEEP), lambda i: (0, at + i))],
        out_shape=[
            jax.ShapeDtypeStruct((D, WIDE), bf16),
            jax.ShapeDtypeStruct((D, WIDE), bf16),
            jax.ShapeDtypeStruct((R, D), bf16),
        ],
        input_output_aliases={4 + k: k for k in range(len(before))},
        compiler_params=params(16),
        cost_estimate=LITTLE,
        name="merge",
    )(tokens, grad, error, q_t, *before, *after)


def pair_sum_body(core_ref, a_ref, b_ref, out_ref):
    s = a_ref[...].astype(f32) + b_ref[...].astype(f32)
    half = R // 2
    out_ref[...] = jnp.where(core_ref[2] == 0, s[:half], s[half:]).astype(bf16)


def add_body(a_ref, b_ref, out_ref):
    out_ref[...] = (a_ref[...].astype(f32) + b_ref[...].astype(f32)).astype(bf16)


def halves_joined(place_ref, mine, theirs):
    a, b = mine[...].astype(f32), theirs[...].astype(f32)
    first = place_ref[2] == 0
    return jnp.concatenate([jnp.where(first, a, b), jnp.where(first, b, a)], axis=0)


def to_core():
    return [(2 * z + c, 2 * z + 1 - c) for z in range(SIDE) for c in range(2)]


def swap(array):
    return lax.ppermute(array, "dp", to_core())


def from_chip(array, second):
    ws = (3, 2, 1, 0) if second else (1, 0, 3, 2)
    to = [(2 * z + c, 2 * w + c) for z, w in enumerate(ws) for c in range(2)]
    return lax.ppermute(array, "dp", to)


def pair_sum(place, local, after=()):
    return pl.pallas_call(
        skipping(pair_sum_body, 3, len(after)),
        in_specs=[SM, VM, VM] + [ANY] * len(after),
        out_specs=VM,
        out_shape=jax.ShapeDtypeStruct((R // 2, local.shape[1]), bf16),
        compiler_params=params(4),
        cost_estimate=LITTLE,
        name="pair_sum",
    )(place, local, swap(local), *after)


def ortho_body(place_ref, mine, theirs, out_ref):
    left = halves_joined(place_ref, mine, theirs) * 0.125
    gram = lax.dot_general(left, left, NT, precision=highest, preferred_element_type=f32)
    row_id = lax.broadcasted_iota(jnp.int32, (R, R), 0)
    col_id = lax.broadcasted_iota(jnp.int32, (R, R), 1)
    work = jnp.concatenate([gram, (row_id == col_id).astype(f32)], axis=1)
    row_ids = lax.broadcasted_iota(jnp.int32, (R, 2 * R), 0)
    for k in range(R):
        scale = lax.rsqrt(work[k : k + 1, k : k + 1])
        row = work[k : k + 1, :] * scale
        col = work[:, k : k + 1] * scale
        work = jnp.where(row_ids > k, work - col * row, jnp.where(row_ids == k, row, work))
    inverse = work[:, R:]
    out_ref[...] = lax.dot_general(
        inverse, left, NN, precision=highest, preferred_element_type=f32
    ).astype(bf16)


def ortho(place, mine, theirs, after=()):
    return pl.pallas_call(
        skipping(ortho_body, 3, len(after)),
        in_specs=[SM, VM, VM] + [ANY] * len(after),
        out_specs=VM,
        out_shape=jax.ShapeDtypeStruct((R, D), bf16),
        compiler_params=params(12),
        cost_estimate=LITTLE,
        name="ortho",
    )(place, mine, theirs, *after)


def right_body(left_ref, high_ref, out_ref, total_ref):
    i = pl.program_id(0)
    term = dot(left_ref[...], high_ref[...], NN)

    @pl.when(i == 0)
    def _():
        total_ref[...] = term

    @pl.when(i > 0)
    def _():
        total_ref[...] += term

    @pl.when(i == D // DEEP - 1)
    def _():
        out_ref[...] = total_ref[...].astype(bf16)


def right(left, high, after=()):
    return pl.pallas_call(
        skipping(right_body, 2, len(after)),
        grid=(D // DEEP,),
        in_specs=[
            pl.BlockSpec((R, DEEP), lambda i: (0, i)),
            pl.BlockSpec((DEEP, WIDE), lambda i: (i, 0)),
        ]
        + [ANY] * len(after),
        out_specs=pl.BlockSpec((R, WIDE), lambda i: (0, 0)),
        out_shape=jax.ShapeDtypeStruct((R, WIDE), bf16),
        scratch_shapes=[pltpu.VMEM((R, WIDE), f32)],
        compiler_params=params(8),
        cost_estimate=LITTLE,
        name="right",
    )(left, high, *after)


def error_body(left_ref, high_ref, low_ref, mine, theirs, q_ref, out_ref):
    q_next = (mine[...].astype(f32) + theirs[...].astype(f32)) * 0.125
    q_ref[...] = q_next
    approx = dot(left_ref[...], q_next.astype(bf16), TN)
    out_ref[0] = (
        (high_ref[...].astype(f32) - approx) + low_ref[...].astype(f32)
    ).astype(bf16)


def error(left, high, low, mine, theirs):
    wide = pl.BlockSpec((DEEP, WIDE), lambda i: (i, 0))
    return pl.pallas_call(
        error_body,
        grid=(D // DEEP,),
        in_specs=[pl.BlockSpec((R, DEEP), lambda i: (0, i)), wide, wide, VM, VM],
        out_specs=[VM, pl.BlockSpec((1, DEEP, WIDE), lambda i: (0, i, 0))],
        out_shape=[
            jax.ShapeDtypeStruct((R, WIDE), f32),
            jax.ShapeDtypeStruct((1, D, WIDE), bf16),
        ],
        compiler_params=params(14),
        cost_estimate=LITTLE,
        name="error",
    )(left, high, low, mine, theirs)


def shards(tokens, gate_weight, up_values, hidden_grad, log_ratios, q_factors, error_feedback):
    spot = lax.axis_index("tensor").astype(jnp.int32)
    core = lax.axis_index("dp").astype(jnp.int32) & 1
    place = jnp.stack([spot & 3, spot >> 2, core])

    def along(axis, y, x, d):
        return ((y + d) % SIDE) * SIDE + x if axis == "y" else y * SIDE + (x + d) % SIDE

    spots = [(y, x) for y in range(SIDE) for x in range(SIDE)]
    n_spots = SIDE * SIDE

    def send(array, axis, d):
        to = [(y * SIDE + x, along(axis, y, x, d)) for y, x in spots]
        return lax.ppermute(array, "tensor", to)

    def send_on(array, axis):
        to = [
            (n_spots * i + y * SIDE + x, n_spots * i + along(axis, y, x, 1 + 2 * (i % 2)))
            for i in range(2 * SIDE)
            for y, x in spots
        ]
        return lax.ppermute(array, ("dp", "tensor"), to)

    in_hbm = lambda array: pltpu.with_memory_space_constraint(array, pltpu.HBM)
    tokens, up_values, hidden_grad, error_feedback = map(
        in_hbm, (tokens, up_values, hidden_grad, error_feedback)
    )
    q_t = q_factors.T

    grad, far_x, far_y, weight = gate(
        place, log_ratios.T, tokens, in_hbm(gate_weight), hidden_grad, up_values
    )
    far_x, far_y = send_on(far_x, "x"), send_on(far_y, "y")
    swapped = swap(grad)
    mine_x, mine_y, own_x, own_y = terms((NEAR, OWN), place, grad, weight)
    near_x, near_y = terms((NEAR,), place, swapped, weight, (mine_x,))
    m = near_x
    near_x, near_y = send_on(near_x, "x"), send_on(near_y, "y")
    high, low, left_local = merge(tokens, grad, error_feedback, q_t, after=(m,))
    message_x = add(mine_x, far_x, (left_local,))
    message_y = add(mine_y, far_y, (message_x,))
    last_x, last_y = send_on(message_x, "x"), send_on(message_y, "y")
    part = pair_sum(place, left_local, (message_y,))
    near_x, near_y, part = lax.optimization_barrier((near_x, near_y, part))
    near_x, near_y = swap(near_x), swap(near_y)
    part = add(part, from_chip(part, False))
    part = add(part, from_chip(part, True))

    def across(axis):
        return "y" if axis == "x" else "x"

    here_x, other_x, this_x, far_x = own("x", place, own_x, last_x, near_x, (part,))
    far_x, other_x = send(far_x, across("x"), 2), swap(other_x)
    here_y, other_y, this_y, far_y = own("y", place, own_y, last_y, near_y, (here_x,))
    far_y, other_y = send(far_y, across("y"), 2), swap(other_y)
    left = ortho(place, part, swap(part), (here_y,))
    right_local = right(left, high, (far_x, far_y))
    part = from_chip(right_local, False)
    next_x = send_on(pack(this_x, other_x, (right_local,)), across("x"))
    next_y = send_on(pack(this_y, other_y, (right_local,)), across("y"))
    part = add(right_local, part)
    part = add(part, from_chip(part, True))
    next_x, next_y, part = lax.optimization_barrier((next_x, next_y, part))
    q_next, error_next = error(left, high, low, part, swap(part))
    across_x = (here_x, far_x, next_x, swap(next_x))
    across_y = (here_y, far_y, next_y, swap(next_y))
    token_grad = pl.pallas_call(
        add_terms,
        in_specs=[VM] * 8,
        out_specs=VM,
        out_shape=jax.ShapeDtypeStruct((ROWS, OUT), bf16),
        compiler_params=params(8),
        cost_estimate=LITTLE,
        name="add_terms",
    )(*across_x, *across_y)
    return (token_grad, q_next.T, error_next)


def solution(mesh):
    return jax.shard_map(
        shards,
        mesh=mesh,
        in_specs=(
            P("dp", None),
            P(None, "tensor"),
            P("dp", "tensor"),
            P("dp", "tensor"),
            P("dp", None),
            P("tensor", None),
            P("dp", None, "tensor"),
        ),
        out_specs=(P("dp", "tensor"), P("tensor", None), P("dp", None, "tensor")),
        check_vma=False,
    )
```

```python
import functools

import jax
import jax.numpy as jnp
from jax import lax
from jax.experimental import pallas as pl
from jax.experimental.pallas import tpu as pltpu
from jax.sharding import PartitionSpec as P

bf16 = jnp.bfloat16
f32 = jnp.float32
MIB = 1 << 20

LEN = 80
PAIR = 2 * LEN
ROWS = 1280
ROWS_A = 640
D = 4096
WIDE = 896
OUT = 256
R = 32
SIDE = 4

dpo_beta = 0.1
highest = lax.Precision.HIGHEST
NT = (((1,), (1,)), ((), ()))
TN = (((0,), (0,)), ((), ()))
NN = (((1,), (0,)), ((), ()))

VM = pl.BlockSpec(memory_space=pltpu.VMEM)
SM = pl.BlockSpec(memory_space=pltpu.SMEM)
ANY = pl.BlockSpec(memory_space=pl.ANY)
HBM = pl.BlockSpec(memory_space=pltpu.HBM)


def params(mib):
    return pltpu.CompilerParams(vmem_limit_bytes=mib * MIB)


LITTLE = pl.CostEstimate(flops=1, bytes_accessed=1, transcendentals=0)


def skipping(body, n, more):
    return lambda *refs: body(*refs[:n], *refs[n + more :])


def dot(a, b, dims):
    return lax.dot_general(a, b, dims, preferred_element_type=f32)


CHUNK = 512
TILE = 2 * PAIR
DEST = SIDE * OUT
GROUPS = (("x", 0, ROWS_A), ("y", ROWS_A, ROWS - ROWS_A))
FAR, NEAR, OWN = range(3)


def position(kind, axis, place_ref):
    me = place_ref[0 if axis == "x" else 1]
    core = place_ref[2]
    return lax.rem(me + (2, 1 + 2 * core, 0)[kind], SIDE)


def weights_for(axis, c, weight_ref):
    if axis == "y":
        return weight_ref[pl.ds(pl.multiple_of(c * DEST, DEST), DEST), :]
    return jnp.concatenate(
        [weight_ref[pl.ds(feature_block(axis, j, c), OUT), :] for j in range(SIDE)], axis=0
    )


def put_terms(kind, place_ref, grad_ref, weight_ref, outs):
    for (axis, base, n), out_ref in zip(GROUPS, outs):
        weight = weights_for(axis, position(kind, axis, place_ref), weight_ref)
        term = dot(grad_ref[base : base + n, :], weight, NT).astype(bf16)
        for j in range(SIDE):
            out_ref[j] = term[:, j * OUT : (j + 1) * OUT]


def feature_block(axis, j, c):
    return pl.multiple_of((j * SIDE + c if axis == "x" else c * SIDE + j) * OUT, OUT)


def gate_grad_of(pair, ratio_ref, gate_pre, hidden, up):
    margin = dpo_beta * (ratio_ref[0:1, :] - ratio_ref[1:2, :])
    scaled = dpo_beta * jax.nn.sigmoid(-margin[:, pair : pair + 1])
    chosen = lax.broadcasted_iota(jnp.int32, (PAIR, 1), 0) < LEN
    row_weight = jnp.where(chosen, -scaled, scaled)
    s = jax.nn.sigmoid(gate_pre)
    slope = s * (1.0 + gate_pre * (1.0 - s))
    return (row_weight * hidden.astype(f32) * up.astype(f32) * slope).astype(bf16)


def gate_body(
    place_ref, ratio_hbm, token_hbm, weight_hbm, hidden_hbm, up_hbm,
    grad_ref, far_x, far_y, weight_ref, token_ref, hidden_ref, up_ref, ratio_ref, pre_ref, sems,
):
    n_chunks, n_tiles = D // CHUNK, ROWS // TILE
    chunks = [slice(k * CHUNK, (k + 1) * CHUNK) for k in range(n_chunks)]
    tiles = [slice(t * TILE, (t + 1) * TILE) for t in range(n_tiles)]
    pairs = [
        (source.at[at], target.at[at])
        for source, target, places in (
            (weight_hbm, weight_ref, [(at,) for at in chunks]),
            (token_hbm, token_ref, [(tiles[0], at) for at in chunks]),
            (token_hbm, token_ref, [(at,) for at in tiles[1:]]),
            (hidden_hbm, hidden_ref, [(at,) for at in tiles]),
            (up_hbm, up_ref, [(at,) for at in tiles]),
        )
        for at in places
    ]
    copies = [pltpu.make_async_copy(*pair, sems.at[i]) for i, pair in enumerate(pairs)]
    weights, first, copies = copies[:n_chunks], copies[n_chunks : 2 * n_chunks], copies[2 * n_chunks :]
    later, hidden, up = copies[: n_tiles - 1], copies[n_tiles - 1 : 2 * n_tiles - 1], copies[2 * n_tiles - 1 :]
    ratios = pltpu.make_async_copy(ratio_hbm, ratio_ref, sems.at[len(pairs)])
    ratios.start()
    for k in range(n_chunks):
        weights[k].start()
        first[k].start()
    for t in range(n_tiles):
        if t:
            later[t - 1].start()
        hidden[t].start()
        up[t].start()


    for t in range(n_tiles):
        if t == 0:
            for k, at in enumerate(chunks):
                weights[k].wait()
                first[k].wait()
                part = dot(token_ref[tiles[0], at], weight_ref[at], NN)
                if k == 0:
                    pre_ref[...] = part
                elif k < n_chunks - 1:
                    pre_ref[...] += part
            gate_pre = pre_ref[...] + part
            ratios.wait()
        else:
            later[t - 1].wait()
            gate_pre = dot(token_ref[tiles[t]], weight_ref[...], NN)
        hidden[t].wait()
        up[t].wait()
        for p in range(TILE // PAIR):
            row = t * TILE + p * PAIR
            at = slice(row, row + PAIR)
            grad_ref[at] = gate_grad_of(
                row // PAIR, ratio_ref, gate_pre[p * PAIR : (p + 1) * PAIR], hidden_ref[at], up_ref[at]
            )
    put_terms(FAR, place_ref, grad_ref, weight_ref, (far_x, far_y))


def messages():
    return [jax.ShapeDtypeStruct((SIDE, n, OUT), bf16) for _, _, n in GROUPS]


def gate(place, ratios, tokens, weight, hidden, up):
    return pl.pallas_call(
        gate_body,
        in_specs=[SM, HBM, HBM, HBM, HBM, HBM],
        out_specs=[VM] * 4,
        out_shape=[jax.ShapeDtypeStruct((ROWS, WIDE), bf16), *messages(), pltpu.VMEM((D, WIDE), bf16)],
        scratch_shapes=[
            pltpu.VMEM((ROWS, D), bf16),
            pltpu.VMEM((ROWS, WIDE), bf16),
            pltpu.VMEM((ROWS, WIDE), bf16),
            pltpu.VMEM((2, ROWS // PAIR), f32),
            pltpu.VMEM((TILE, WIDE), f32),
            pltpu.SemaphoreType.DMA((2 * (D // CHUNK) + 3 * (ROWS // TILE),)),
        ],
        compiler_params=params(30),
        cost_estimate=LITTLE,
        name="gate",
    )(place, ratios, tokens, weight, hidden, up)


def terms(kinds, place, grad, weight, after=()):
    def body(place_ref, grad_ref, weight_ref, *refs):
        outs = refs[len(after) :]
        for i, kind in enumerate(kinds):
            put_terms(kind, place_ref, grad_ref, weight_ref, outs[2 * i : 2 * i + 2])

    return pl.pallas_call(
        body,
        in_specs=[SM, VM, VM] + [ANY] * len(after),
        out_specs=[VM] * 2 * len(kinds),
        out_shape=messages() * len(kinds),
        compiler_params=params(16),
        cost_estimate=LITTLE,
        name="terms",
    )(place, grad, weight, *after)


def add(a, b, after=()):
    return pl.pallas_call(
        skipping(add_body, 2, len(after)),
        in_specs=[VM, VM] + [ANY] * len(after),
        out_specs=VM,
        out_shape=jax.ShapeDtypeStruct(a.shape, bf16),
        compiler_params=params(6),
        cost_estimate=LITTLE,
        name="add",
    )(a, b, *after)


def own_body(axis, place_ref, a_ref, b_ref, c_ref, here, other_way, this_way, far):
    me, core = place_ref[1 if axis == "x" else 0], place_ref[2]
    for d, out_ref in ((0, here), (3 - 2 * core, other_way), (1 + 2 * core, this_way), (2, far)):
        j = lax.rem(me + d, SIDE)
        out_ref[...] = (
            a_ref[j].astype(f32) + b_ref[j].astype(f32) + c_ref[j].astype(f32)
        ).astype(bf16)


def own(axis, place, a, b, c, after=()):
    n = a.shape[1]
    return pl.pallas_call(
        skipping(functools.partial(own_body, axis), 4, len(after)),
        in_specs=[SM] + [VM] * 3 + [ANY] * len(after),
        out_specs=[VM] * SIDE,
        out_shape=[jax.ShapeDtypeStruct((n, OUT), bf16)] * SIDE,
        compiler_params=params(8),
        cost_estimate=LITTLE,
        name="own_" + axis,
    )(place, a, b, c, *after)


def pack_body(a_ref, b_ref, out_ref):
    out_ref[0] = a_ref[...]
    out_ref[1] = b_ref[...]


def pack(a, b, after=()):
    return pl.pallas_call(
        skipping(pack_body, 2, len(after)),
        in_specs=[VM, VM] + [ANY] * len(after),
        out_specs=VM,
        out_shape=jax.ShapeDtypeStruct((2, *a.shape), bf16),
        compiler_params=params(4),
        cost_estimate=LITTLE,
        name="pack",
    )(a, b, *after)


def add_terms(*refs):
    out_ref = refs[-1]
    for g, (_, base, n) in enumerate(GROUPS):
        here, far, near, theirs = refs[4 * g : 4 * g + 4]
        parts = [r.astype(f32) for r in (here[...], far[...], near[0], theirs[1])]
        out_ref[base : base + n] = ((parts[0] + parts[1]) + (parts[2] + parts[3])).astype(bf16)


DEEP = 512


def merge_body(token_ref, grad_ref, error_ref, q_ref, high_ref, low_ref, left_ref):
    at = pl.ds(pl.multiple_of(pl.program_id(0) * DEEP, DEEP), DEEP)
    m = dot(token_ref[...], grad_ref[...], TN) + error_ref[0].astype(f32)
    high = m.astype(bf16)
    high_ref[at] = high
    low_ref[at] = (m - high.astype(f32)).astype(bf16)
    left_ref[...] = dot(q_ref[...].astype(bf16), high, NT).astype(bf16)


def merge(tokens, grad, error, q_t, after=()):
    return pl.pallas_call(
        skipping(merge_body, 4, len(after)),
        grid=(D // DEEP,),
        in_specs=[
            pl.BlockSpec((ROWS, DEEP), lambda i: (0, i)),
            VM,
            pl.BlockSpec((1, DEEP, WIDE), lambda i: (0, i, 0)),
            VM,
        ]
        + [ANY] * len(after),
        out_specs=[VM, VM, pl.BlockSpec((R, DEEP), lambda i: (0, i))],
        out_shape=[
            pltpu.VMEM((D, WIDE), bf16),
            pltpu.VMEM((D, WIDE), bf16),
            jax.ShapeDtypeStruct((R, D), bf16),
        ],
        compiler_params=params(14),
        cost_estimate=LITTLE,
        name="merge",
    )(tokens, grad, error, q_t, *after)


def pair_sum_body(core_ref, a_ref, b_ref, out_ref):
    s = a_ref[...].astype(f32) + b_ref[...].astype(f32)
    half = R // 2
    out_ref[...] = jnp.where(core_ref[2] == 0, s[:half], s[half:]).astype(bf16)


def add_body(a_ref, b_ref, out_ref):
    out_ref[...] = (a_ref[...].astype(f32) + b_ref[...].astype(f32)).astype(bf16)


def halves_joined(place_ref, mine, theirs):
    a, b = mine[...].astype(f32), theirs[...].astype(f32)
    first = place_ref[2] == 0
    return jnp.concatenate([jnp.where(first, a, b), jnp.where(first, b, a)], axis=0)


def to_core():
    return [(2 * z + c, 2 * z + 1 - c) for z in range(SIDE) for c in range(2)]


def swap(array):
    return lax.ppermute(array, "dp", to_core())


def from_chip(array, d):
    to = [(2 * z + c, 2 * ((z + d) % SIDE) + c) for z in range(SIDE) for c in range(2)]
    return lax.ppermute(array, "dp", to)


def from_neighbour(array, second):
    ws = (3, 2, 1, 0) if second else (1, 0, 3, 2)
    to = [(2 * z + c, 2 * w + c) for z, w in enumerate(ws) for c in range(2)]
    return lax.ppermute(array, "dp", to)


def chips_sum_body(a_ref, b_ref, c_ref, d_ref, out_ref):
    a, b, c, d = (r[...].astype(f32) for r in (a_ref, b_ref, c_ref, d_ref))
    out_ref[...] = ((a + c) + (b + d)).astype(bf16)


def chips_sum(arrays, after=()):
    return pl.pallas_call(
        skipping(chips_sum_body, SIDE, len(after)),
        in_specs=[VM] * SIDE + [ANY] * len(after),
        out_specs=VM,
        out_shape=jax.ShapeDtypeStruct(arrays[0].shape, bf16),
        compiler_params=params(4),
        cost_estimate=LITTLE,
        name="chips_sum",
    )(*arrays, *after)


def pair_sum(place, local, after=()):
    return pl.pallas_call(
        skipping(pair_sum_body, 3, len(after)),
        in_specs=[SM, VM, VM] + [ANY] * len(after),
        out_specs=VM,
        out_shape=jax.ShapeDtypeStruct((R // 2, local.shape[1]), bf16),
        compiler_params=params(4),
        cost_estimate=LITTLE,
        name="pair_sum",
    )(place, local, swap(local), *after)


def ortho_body(place_ref, mine, theirs, out_ref):
    left = (halves_joined(place_ref, mine, theirs) * 0.125).astype(bf16)
    gram = dot(left, left, NT)
    row_id = lax.broadcasted_iota(jnp.int32, (R, R), 0)
    eye = row_id == lax.broadcasted_iota(jnp.int32, (R, R), 1)
    work = jnp.concatenate([gram, eye.astype(f32)], axis=1)
    below = lax.broadcasted_iota(jnp.int32, (R, 1), 0)
    for k in range(R - 1):
        col = jnp.where(below > k, work[:, k : k + 1], 0.0)
        work -= (col * (1.0 / work[k : k + 1, k : k + 1])) * work[k : k + 1, :]
    pivots = jnp.sum(jnp.where(eye, work[:, :R], 0.0), axis=1, keepdims=True)
    inverse = work[:, R:] * lax.rsqrt(pivots)
    parts = []
    for _ in range(3):
        parts.append(inverse.astype(bf16))
        inverse -= parts[-1].astype(f32)
    product = dot(jnp.concatenate(parts, axis=0), left, NN)
    out_ref[...] = (
        product[:R] + (product[R : 2 * R] + product[2 * R :])
    ).astype(bf16)


def ortho(place, mine, theirs, after=()):
    return pl.pallas_call(
        skipping(ortho_body, 3, len(after)),
        in_specs=[SM, VM, VM] + [ANY] * len(after),
        out_specs=VM,
        out_shape=jax.ShapeDtypeStruct((R, D), bf16),
        compiler_params=params(12),
        cost_estimate=LITTLE,
        name="ortho",
    )(place, mine, theirs, *after)


def right_body(left_ref, high_ref, out_ref):
    total = jnp.zeros((R, WIDE), f32)
    for i in range(D // DEEP):
        at = slice(i * DEEP, (i + 1) * DEEP)
        total += dot(left_ref[:, at], high_ref[at], NN)
    out_ref[...] = total.astype(bf16)


def right(left, high, after=()):
    return pl.pallas_call(
        skipping(right_body, 2, len(after)),
        in_specs=[VM, VM] + [ANY] * len(after),
        out_specs=VM,
        out_shape=jax.ShapeDtypeStruct((R, WIDE), bf16),
        compiler_params=params(8),
        cost_estimate=LITTLE,
        name="right",
    )(left, high, *after)


def error_body(left_ref, high_ref, low_ref, mine, theirs, q_ref, error_hbm, error_ref, sems):
    q_next = (mine[...].astype(f32) + theirs[...].astype(f32)) * 0.125
    q_ref[...] = q_next
    q_round = q_next.astype(bf16)
    copies = []
    for i in range(D // DEEP):
        at = pl.ds(i * DEEP, DEEP)
        approx = dot(left_ref[:, at], q_round, TN)
        error_ref[at] = (
            (high_ref[at].astype(f32) - approx) + low_ref[at].astype(f32)
        ).astype(bf16)
        copies.append(pltpu.make_async_copy(error_ref.at[at], error_hbm.at[0, at], sems.at[i]))
        copies[-1].start()
    for copy in copies:
        copy.wait()


def error(left, high, low, mine, theirs):
    return pl.pallas_call(
        error_body,
        in_specs=[VM] * 5,
        out_specs=[VM, HBM],
        out_shape=[
            jax.ShapeDtypeStruct((R, WIDE), f32),
            jax.ShapeDtypeStruct((1, D, WIDE), bf16),
        ],
        scratch_shapes=[pltpu.VMEM((D, WIDE), bf16), pltpu.SemaphoreType.DMA((D // DEEP,))],
        compiler_params=params(14),
        cost_estimate=LITTLE,
        name="error",
    )(left, high, low, mine, theirs)


def shards(tokens, gate_weight, up_values, hidden_grad, log_ratios, q_factors, error_feedback):
    spot = lax.axis_index("tensor").astype(jnp.int32)
    core = lax.axis_index("dp").astype(jnp.int32) & 1
    place = jnp.stack([spot & 3, spot >> 2, core])

    def along(axis, y, x, d):
        return ((y + d) % SIDE) * SIDE + x if axis == "y" else y * SIDE + (x + d) % SIDE

    spots = [(y, x) for y in range(SIDE) for x in range(SIDE)]
    n_spots = SIDE * SIDE

    def send(array, axis, d):
        to = [(y * SIDE + x, along(axis, y, x, d)) for y, x in spots]
        return lax.ppermute(array, "tensor", to)

    def send_on(array, axis):
        to = [
            (n_spots * i + y * SIDE + x, n_spots * i + along(axis, y, x, 1 + 2 * (i % 2)))
            for i in range(2 * SIDE)
            for y, x in spots
        ]
        return lax.ppermute(array, ("dp", "tensor"), to)

    in_hbm = lambda array: pltpu.with_memory_space_constraint(array, pltpu.HBM)
    tokens, up_values, hidden_grad, error_feedback = map(
        in_hbm, (tokens, up_values, hidden_grad, error_feedback)
    )
    q_t = q_factors.T

    grad, far_x, far_y, weight = gate(
        place, in_hbm(log_ratios.T), tokens, in_hbm(gate_weight), hidden_grad, up_values
    )
    far_x, far_y = send_on(far_x, "x"), send_on(far_y, "y")
    swapped = swap(grad)
    mine_x, mine_y, own_x, own_y = terms((NEAR, OWN), place, grad, weight)
    m, near_y = terms((NEAR,), place, swapped, weight, (mine_x,))
    near_x, near_y = send_on(m, "x"), send_on(near_y, "y")
    high, low, left_local = merge(tokens, grad, error_feedback, q_t, (m,))
    message_x = add(mine_x, far_x, (left_local,))
    message_y = add(mine_y, far_y, (message_x,))
    last_x, last_y = send_on(message_x, "x"), send_on(message_y, "y")
    part = pair_sum(place, left_local, (message_y,))
    near_x, near_y, part = lax.optimization_barrier((near_x, near_y, part))
    near_x, near_y = swap(near_x), swap(near_y)
    part = add(part, from_neighbour(part, False))
    part = add(part, from_neighbour(part, True))

    def across(axis):
        return "y" if axis == "x" else "x"

    here_x, other_x, this_x, far_x = own("x", place, own_x, last_x, near_x, (part,))
    far_x, other_x = send(far_x, across("x"), 2), swap(other_x)
    here_y, other_y, this_y, far_y = own("y", place, own_y, last_y, near_y, (here_x,))
    far_y, other_y = send(far_y, across("y"), 2), swap(other_y)
    left = ortho(place, part, swap(part), (here_y,))
    part = right(left, high)
    next_x = send_on(pack(this_x, other_x, (part, far_x)), across("x"))
    next_y = send_on(pack(this_y, other_y, (part, far_y)), across("y"))
    part = chips_sum((part, from_chip(part, 1), from_chip(part, 2), from_chip(part, 3)))
    theirs = swap(part)
    next_x, next_y, theirs = lax.optimization_barrier((next_x, next_y, theirs))
    q_next, error_next = error(left, high, low, part, theirs)
    across_x = (here_x, far_x, next_x, swap(next_x))
    across_y = (here_y, far_y, next_y, swap(next_y))
    token_grad = pl.pallas_call(
        add_terms,
        in_specs=[VM] * 8,
        out_specs=VM,
        out_shape=jax.ShapeDtypeStruct((ROWS, OUT), bf16),
        compiler_params=params(8),
        cost_estimate=LITTLE,
        name="add_terms",
    )(*across_x, *across_y)
    return (token_grad, q_next.T, error_next)


def solution(mesh):
    return jax.shard_map(
        shards,
        mesh=mesh,
        in_specs=(
            P("dp", None),
            P(None, "tensor"),
            P("dp", "tensor"),
            P("dp", "tensor"),
            P("dp", None),
            P("tensor", None),
            P("dp", None, "tensor"),
        ),
        out_specs=(P("dp", "tensor"), P("tensor", None), P("dp", None, "tensor")),
        check_vma=False,
    )
```

```python
import functools

import jax
import jax.numpy as jnp
from jax import lax
from jax.experimental import pallas as pl
from jax.experimental.pallas import tpu as pltpu
from jax.sharding import PartitionSpec as P

bf16 = jnp.bfloat16
f32 = jnp.float32
MIB = 1 << 20

LEN = 80
PAIR = 2 * LEN
ROWS = 1280
ROWS_A = 640
D = 4096
WIDE = 896
OUT = 256
R = 32
SIDE = 4

dpo_beta = 0.1
highest = lax.Precision.HIGHEST
NT = (((1,), (1,)), ((), ()))
TN = (((0,), (0,)), ((), ()))
NN = (((1,), (0,)), ((), ()))

VM = pl.BlockSpec(memory_space=pltpu.VMEM)
SM = pl.BlockSpec(memory_space=pltpu.SMEM)
ANY = pl.BlockSpec(memory_space=pl.ANY)
HBM = pl.BlockSpec(memory_space=pltpu.HBM)


def params(mib):
    return pltpu.CompilerParams(vmem_limit_bytes=mib * MIB)


LITTLE = pl.CostEstimate(flops=1, bytes_accessed=1, transcendentals=0)


def skipping(body, n, more):
    return lambda *refs: body(*refs[:n], *refs[n + more :])


def dot(a, b, dims):
    return lax.dot_general(a, b, dims, preferred_element_type=f32)


CHUNK = 512
TILE = 2 * PAIR
DEST = SIDE * OUT
GROUPS = (("x", 0, ROWS_A), ("y", ROWS_A, ROWS - ROWS_A))
FAR, NEAR, OWN = range(3)


def position(kind, axis, place_ref):
    me = place_ref[0 if axis == "x" else 1]
    core = place_ref[2]
    return lax.rem(me + (2, 1 + 2 * core, 0)[kind], SIDE)


def weights_for(axis, c, weight_ref):
    if axis == "y":
        return weight_ref[pl.ds(pl.multiple_of(c * DEST, DEST), DEST), :]
    return jnp.concatenate(
        [weight_ref[pl.ds(feature_block(axis, j, c), OUT), :] for j in range(SIDE)], axis=0
    )


def put_terms(kind, place_ref, grad_ref, weight_ref, outs):
    for (axis, base, n), out_ref in zip(GROUPS, outs):
        weight = weights_for(axis, position(kind, axis, place_ref), weight_ref)
        term = dot(grad_ref[base : base + n, :], weight, NT).astype(bf16)
        for j in range(SIDE):
            out_ref[j] = term[:, j * OUT : (j + 1) * OUT]


def feature_block(axis, j, c):
    return pl.multiple_of((j * SIDE + c if axis == "x" else c * SIDE + j) * OUT, OUT)


def gate_grad_of(pair, ratio_ref, gate_pre, hidden, up):
    margin = dpo_beta * (ratio_ref[0:1, :] - ratio_ref[1:2, :])
    scaled = dpo_beta * jax.nn.sigmoid(-margin[:, pair : pair + 1])
    chosen = lax.broadcasted_iota(jnp.int32, (PAIR, 1), 0) < LEN
    row_weight = jnp.where(chosen, -scaled, scaled)
    s = jax.nn.sigmoid(gate_pre)
    slope = s * (1.0 + gate_pre * (1.0 - s))
    return (row_weight * hidden.astype(f32) * up.astype(f32) * slope).astype(bf16)


def gate_body(
    place_ref, ratio_hbm, token_hbm, weight_hbm, hidden_hbm, up_hbm,
    grad_ref, far_x, far_y, weight_ref, token_ref, hidden_ref, up_ref, ratio_ref, pre_ref, sems,
):
    n_chunks, n_tiles = D // CHUNK, ROWS // TILE
    chunks = [slice(k * CHUNK, (k + 1) * CHUNK) for k in range(n_chunks)]
    tiles = [slice(t * TILE, (t + 1) * TILE) for t in range(n_tiles)]
    pairs = [
        (source.at[at], target.at[at])
        for source, target, places in (
            (weight_hbm, weight_ref, [(at,) for at in chunks]),
            (token_hbm, token_ref, [(tiles[0], at) for at in chunks]),
            (token_hbm, token_ref, [(at,) for at in tiles[1:]]),
            (hidden_hbm, hidden_ref, [(at,) for at in tiles]),
            (up_hbm, up_ref, [(at,) for at in tiles]),
        )
        for at in places
    ]
    copies = [pltpu.make_async_copy(*pair, sems.at[i]) for i, pair in enumerate(pairs)]
    weights, first, copies = copies[:n_chunks], copies[n_chunks : 2 * n_chunks], copies[2 * n_chunks :]
    later, hidden, up = copies[: n_tiles - 1], copies[n_tiles - 1 : 2 * n_tiles - 1], copies[2 * n_tiles - 1 :]
    ratios = pltpu.make_async_copy(ratio_hbm, ratio_ref, sems.at[len(pairs)])
    ratios.start()
    for k in range(n_chunks):
        weights[k].start()
        first[k].start()
    for t in range(n_tiles):
        if t:
            later[t - 1].start()
        hidden[t].start()
        up[t].start()


    for t in range(n_tiles):
        if t == 0:
            for k, at in enumerate(chunks):
                weights[k].wait()
                first[k].wait()
                part = dot(token_ref[tiles[0], at], weight_ref[at], NN)
                if k == 0:
                    pre_ref[...] = part
                elif k < n_chunks - 1:
                    pre_ref[...] += part
            gate_pre = pre_ref[...] + part
            ratios.wait()
        else:
            later[t - 1].wait()
            gate_pre = dot(token_ref[tiles[t]], weight_ref[...], NN)
        hidden[t].wait()
        up[t].wait()
        for p in range(TILE // PAIR):
            row = t * TILE + p * PAIR
            at = slice(row, row + PAIR)
            grad_ref[at] = gate_grad_of(
                row // PAIR, ratio_ref, gate_pre[p * PAIR : (p + 1) * PAIR], hidden_ref[at], up_ref[at]
            )
    put_terms(FAR, place_ref, grad_ref, weight_ref, (far_x, far_y))


def messages():
    return [jax.ShapeDtypeStruct((SIDE, n, OUT), bf16) for _, _, n in GROUPS]


def gate(place, ratios, tokens, weight, hidden, up):
    return pl.pallas_call(
        gate_body,
        in_specs=[SM, HBM, HBM, HBM, HBM, HBM],
        out_specs=[VM] * 4,
        out_shape=[jax.ShapeDtypeStruct((ROWS, WIDE), bf16), *messages(), pltpu.VMEM((D, WIDE), bf16)],
        scratch_shapes=[
            pltpu.VMEM((ROWS, D), bf16),
            pltpu.VMEM((ROWS, WIDE), bf16),
            pltpu.VMEM((ROWS, WIDE), bf16),
            pltpu.VMEM((2, ROWS // PAIR), f32),
            pltpu.VMEM((TILE, WIDE), f32),
            pltpu.SemaphoreType.DMA((2 * (D // CHUNK) + 3 * (ROWS // TILE),)),
        ],
        compiler_params=params(30),
        cost_estimate=LITTLE,
        name="gate",
    )(place, ratios, tokens, weight, hidden, up)


def terms(kinds, place, grad, weight, after=()):
    def body(place_ref, grad_ref, weight_ref, *refs):
        outs = refs[len(after) :]
        for i, kind in enumerate(kinds):
            put_terms(kind, place_ref, grad_ref, weight_ref, outs[2 * i : 2 * i + 2])

    return pl.pallas_call(
        body,
        in_specs=[SM, VM, VM] + [ANY] * len(after),
        out_specs=[VM] * 2 * len(kinds),
        out_shape=messages() * len(kinds),
        compiler_params=params(16),
        cost_estimate=LITTLE,
        name="terms",
    )(place, grad, weight, *after)


def add(a, b, after=()):
    return pl.pallas_call(
        skipping(add_body, 2, len(after)),
        in_specs=[VM, VM] + [ANY] * len(after),
        out_specs=VM,
        out_shape=jax.ShapeDtypeStruct(a.shape, bf16),
        compiler_params=params(6),
        cost_estimate=LITTLE,
        name="add",
    )(a, b, *after)


def own_body(axis, place_ref, a_ref, b_ref, c_ref, here, other_way, this_way, far):
    me, core = place_ref[1 if axis == "x" else 0], place_ref[2]
    for d, out_ref in ((0, here), (3 - 2 * core, other_way), (1 + 2 * core, this_way), (2, far)):
        j = lax.rem(me + d, SIDE)
        out_ref[...] = (
            a_ref[j].astype(f32) + b_ref[j].astype(f32) + c_ref[j].astype(f32)
        ).astype(bf16)


def own(axis, place, a, b, c, after=()):
    n = a.shape[1]
    return pl.pallas_call(
        skipping(functools.partial(own_body, axis), 4, len(after)),
        in_specs=[SM] + [VM] * 3 + [ANY] * len(after),
        out_specs=[VM] * SIDE,
        out_shape=[jax.ShapeDtypeStruct((n, OUT), bf16)] * SIDE,
        compiler_params=params(8),
        cost_estimate=LITTLE,
        name="own_" + axis,
    )(place, a, b, c, *after)


def pack_body(a_ref, b_ref, out_ref):
    out_ref[0] = a_ref[...]
    out_ref[1] = b_ref[...]


def pack(a, b, after=()):
    return pl.pallas_call(
        skipping(pack_body, 2, len(after)),
        in_specs=[VM, VM] + [ANY] * len(after),
        out_specs=VM,
        out_shape=jax.ShapeDtypeStruct((2, *a.shape), bf16),
        compiler_params=params(4),
        cost_estimate=LITTLE,
        name="pack",
    )(a, b, *after)


def add_terms(*refs):
    out_ref = refs[-1]
    for g, (_, base, n) in enumerate(GROUPS):
        here, far, near, theirs = refs[4 * g : 4 * g + 4]
        parts = [r.astype(f32) for r in (here[...], far[...], near[0], theirs[1])]
        out_ref[base : base + n] = ((parts[0] + parts[1]) + (parts[2] + parts[3])).astype(bf16)


DEEP = 512


def merge_body(token_ref, grad_ref, error_ref, q_ref, high_ref, low_ref, left_ref):
    at = pl.ds(pl.multiple_of(pl.program_id(0) * DEEP, DEEP), DEEP)
    m = dot(token_ref[...], grad_ref[...], TN) + error_ref[0].astype(f32)
    high = m.astype(bf16)
    high_ref[at] = high
    low_ref[at] = (m - high.astype(f32)).astype(bf16)
    left_ref[...] = dot(q_ref[...].astype(bf16), high, NT).astype(bf16)


def merge(tokens, grad, error, q_t, after=()):
    return pl.pallas_call(
        skipping(merge_body, 4, len(after)),
        grid=(D // DEEP,),
        in_specs=[
            pl.BlockSpec((ROWS, DEEP), lambda i: (0, i)),
            VM,
            pl.BlockSpec((1, DEEP, WIDE), lambda i: (0, i, 0)),
            VM,
        ]
        + [ANY] * len(after),
        out_specs=[VM, VM, pl.BlockSpec((R, DEEP), lambda i: (0, i))],
        out_shape=[
            pltpu.VMEM((D, WIDE), bf16),
            pltpu.VMEM((D, WIDE), bf16),
            jax.ShapeDtypeStruct((R, D), bf16),
        ],
        compiler_params=params(14),
        cost_estimate=LITTLE,
        name="merge",
    )(tokens, grad, error, q_t, *after)


def pair_sum_body(core_ref, a_ref, b_ref, out_ref):
    s = a_ref[...].astype(f32) + b_ref[...].astype(f32)
    half = R // 2
    out_ref[...] = jnp.where(core_ref[2] == 0, s[:half], s[half:]).astype(bf16)


def add_body(a_ref, b_ref, out_ref):
    out_ref[...] = (a_ref[...].astype(f32) + b_ref[...].astype(f32)).astype(bf16)


def halves_joined(place_ref, mine, theirs):
    a, b = mine[...].astype(f32), theirs[...].astype(f32)
    first = place_ref[2] == 0
    return jnp.concatenate([jnp.where(first, a, b), jnp.where(first, b, a)], axis=0)


def to_core():
    return [(2 * z + c, 2 * z + 1 - c) for z in range(SIDE) for c in range(2)]


def swap(array):
    return lax.ppermute(array, "dp", to_core())


def from_neighbour(array, second):
    ws = (3, 2, 1, 0) if second else (1, 0, 3, 2)
    to = [(2 * z + c, 2 * w + c) for z, w in enumerate(ws) for c in range(2)]
    return lax.ppermute(array, "dp", to)


def pair_sum(place, local, after=()):
    return pl.pallas_call(
        skipping(pair_sum_body, 3, len(after)),
        in_specs=[SM, VM, VM] + [ANY] * len(after),
        out_specs=VM,
        out_shape=jax.ShapeDtypeStruct((R // 2, local.shape[1]), bf16),
        compiler_params=params(4),
        cost_estimate=LITTLE,
        name="pair_sum",
    )(place, local, swap(local), *after)


def ortho_body(place_ref, mine, theirs, out_ref):
    left = (halves_joined(place_ref, mine, theirs) * 0.125).astype(bf16)
    gram = dot(left, left, NT)
    row_id = lax.broadcasted_iota(jnp.int32, (R, R), 0)
    eye = row_id == lax.broadcasted_iota(jnp.int32, (R, R), 1)
    work = jnp.concatenate([gram, eye.astype(f32)], axis=1)
    below = lax.broadcasted_iota(jnp.int32, (R, 1), 0)
    for k in range(R - 1):
        col = jnp.where(below > k, work[:, k : k + 1], 0.0)
        work -= (col * (1.0 / work[k : k + 1, k : k + 1])) * work[k : k + 1, :]
    pivots = jnp.sum(jnp.where(eye, work[:, :R], 0.0), axis=1, keepdims=True)
    inverse = work[:, R:] * lax.rsqrt(pivots)
    parts = []
    for _ in range(3):
        parts.append(inverse.astype(bf16))
        inverse -= parts[-1].astype(f32)
    product = dot(jnp.concatenate(parts, axis=0), left, NN)
    out_ref[...] = (
        product[:R] + (product[R : 2 * R] + product[2 * R :])
    ).astype(bf16)


def ortho(place, mine, theirs, after=()):
    return pl.pallas_call(
        skipping(ortho_body, 3, len(after)),
        in_specs=[SM, VM, VM] + [ANY] * len(after),
        out_specs=VM,
        out_shape=jax.ShapeDtypeStruct((R, D), bf16),
        compiler_params=params(12),
        cost_estimate=LITTLE,
        name="ortho",
    )(place, mine, theirs, *after)


def right_body(left_ref, high_ref, out_ref):
    total = jnp.zeros((R, WIDE), f32)
    for i in range(D // DEEP):
        at = slice(i * DEEP, (i + 1) * DEEP)
        total += dot(left_ref[:, at], high_ref[at], NN)
    out_ref[...] = total.astype(bf16)


def right(left, high, after=()):
    return pl.pallas_call(
        skipping(right_body, 2, len(after)),
        in_specs=[VM, VM] + [ANY] * len(after),
        out_specs=VM,
        out_shape=jax.ShapeDtypeStruct((R, WIDE), bf16),
        compiler_params=params(8),
        cost_estimate=LITTLE,
        name="right",
    )(left, high, *after)


def error_body(left_ref, high_ref, low_ref, mine, theirs, q_ref, error_hbm, error_ref, sems):
    q_next = (mine[...].astype(f32) + theirs[...].astype(f32)) * 0.125
    q_ref[...] = q_next
    q_round = q_next.astype(bf16)
    copies = []
    for i in range(D // DEEP):
        at = pl.ds(i * DEEP, DEEP)
        approx = dot(left_ref[:, at], q_round, TN)
        error_ref[at] = (
            (high_ref[at].astype(f32) - approx) + low_ref[at].astype(f32)
        ).astype(bf16)
        copies.append(pltpu.make_async_copy(error_ref.at[at], error_hbm.at[0, at], sems.at[i]))
        copies[-1].start()
    for copy in copies:
        copy.wait()


def error(left, high, low, mine, theirs):
    return pl.pallas_call(
        error_body,
        in_specs=[VM] * 5,
        out_specs=[VM, HBM],
        out_shape=[
            jax.ShapeDtypeStruct((R, WIDE), f32),
            jax.ShapeDtypeStruct((1, D, WIDE), bf16),
        ],
        scratch_shapes=[pltpu.VMEM((D, WIDE), bf16), pltpu.SemaphoreType.DMA((D // DEEP,))],
        compiler_params=params(14),
        cost_estimate=LITTLE,
        name="error",
    )(left, high, low, mine, theirs)


def shards(tokens, gate_weight, up_values, hidden_grad, log_ratios, q_factors, error_feedback):
    spot = lax.axis_index("tensor").astype(jnp.int32)
    core = lax.axis_index("dp").astype(jnp.int32) & 1
    place = jnp.stack([spot & 3, spot >> 2, core])

    def along(axis, y, x, d):
        return ((y + d) % SIDE) * SIDE + x if axis == "y" else y * SIDE + (x + d) % SIDE

    spots = [(y, x) for y in range(SIDE) for x in range(SIDE)]
    n_spots = SIDE * SIDE

    def send(array, axis, d):
        to = [(y * SIDE + x, along(axis, y, x, d)) for y, x in spots]
        return lax.ppermute(array, "tensor", to)

    def send_on(array, axis):
        to = [
            (n_spots * i + y * SIDE + x, n_spots * i + along(axis, y, x, 1 + 2 * (i % 2)))
            for i in range(2 * SIDE)
            for y, x in spots
        ]
        return lax.ppermute(array, ("dp", "tensor"), to)

    in_hbm = lambda array: pltpu.with_memory_space_constraint(array, pltpu.HBM)
    tokens, up_values, hidden_grad, error_feedback = map(
        in_hbm, (tokens, up_values, hidden_grad, error_feedback)
    )
    q_t = q_factors.T

    grad, far_x, far_y, weight = gate(
        place, in_hbm(log_ratios.T), tokens, in_hbm(gate_weight), hidden_grad, up_values
    )
    far_x, far_y = send_on(far_x, "x"), send_on(far_y, "y")
    swapped = swap(grad)
    mine_x, mine_y, own_x, own_y = terms((NEAR, OWN), place, grad, weight)
    m, near_y = terms((NEAR,), place, swapped, weight, (mine_x,))
    near_x, near_y = send_on(m, "x"), send_on(near_y, "y")
    high, low, left_local = merge(tokens, grad, error_feedback, q_t, (m,))
    message_x = add(mine_x, far_x, (left_local,))
    message_y = add(mine_y, far_y, (message_x,))
    last_x, last_y = send_on(message_x, "x"), send_on(message_y, "y")
    part = pair_sum(place, left_local, (message_y,))
    near_x, near_y, part = lax.optimization_barrier((near_x, near_y, part))
    near_x, near_y = swap(near_x), swap(near_y)
    part = add(part, from_neighbour(part, False))
    part = add(part, from_neighbour(part, True))

    theirs = swap(part)

    def across(axis):
        return "y" if axis == "x" else "x"

    here_x, other_x, this_x, far_x = own("x", place, own_x, last_x, near_x, (theirs,))
    far_x, other_x = send(far_x, across("x"), 2), swap(other_x)
    here_y, other_y, this_y, far_y = own("y", place, own_y, last_y, near_y, (here_x,))
    far_y, other_y = send(far_y, across("y"), 2), swap(other_y)
    left = ortho(place, part, theirs, (here_y,))
    part = right(left, high)
    next_x = send_on(pack(this_x, other_x, (part,)), across("x"))
    next_y = send_on(pack(this_y, other_y, (part,)), across("y"))
    part = add(part, from_neighbour(part, False))
    part = add(part, from_neighbour(part, True))
    theirs = swap(part)
    next_x, next_y, theirs = lax.optimization_barrier((next_x, next_y, theirs))
    q_next, error_next = error(left, high, low, part, theirs)
    across_x = (here_x, far_x, next_x, swap(next_x))
    across_y = (here_y, far_y, next_y, swap(next_y))
    token_grad = pl.pallas_call(
        add_terms,
        in_specs=[VM] * 8,
        out_specs=VM,
        out_shape=jax.ShapeDtypeStruct((ROWS, OUT), bf16),
        compiler_params=params(8),
        cost_estimate=LITTLE,
        name="add_terms",
    )(*across_x, *across_y)
    return (token_grad, q_next.T, error_next)


def solution(mesh):
    return jax.shard_map(
        shards,
        mesh=mesh,
        in_specs=(
            P("dp", None),
            P(None, "tensor"),
            P("dp", "tensor"),
            P("dp", "tensor"),
            P("dp", None),
            P("tensor", None),
            P("dp", None, "tensor"),
        ),
        out_specs=(P("dp", "tensor"), P("tensor", None), P("dp", None, "tensor")),
        check_vma=False,
    )
```
